32 devices in a mesh: rep: 2 (over x), ep: 16 (over z, y, core).
Axes of the slice: x: 2, y: 2, z: 4, core: 2. Of those that a mesh axis runs over, the one named last changes fastest.
Arguments:
- tokens: bfloat16 [32, 7168], P(('rep', 'ep')), parts along dimension 0, may hold values from -3 to 3
- ffn_gain: float32 [7168], replicated, may hold values from 0.1 to 1.9
- gate_weight: bfloat16 [7168, 9216], P(None, 'ep'), may hold values from -0.0625 to 0.0625
- up_weight: bfloat16 [7168, 9216], P(None, 'ep'), may hold values from -0.0625 to 0.0625
- down_weight: bfloat16 [9216, 7168], P('ep'), may hold values from -0.0625 to 0.0625
- queries: bfloat16 [32, 128, 576], P(('rep', 'ep')), parts along dimension 0, may hold values from -14 to 14
- kv_cache: bfloat16 [32, 1024, 576], P(('rep', 'ep')), parts along dimension 0, may hold values from -6 to 6
- new_kv: bfloat16 [32, 576], P(('rep', 'ep')), parts along dimension 0, may hold values from -6 to 6
- lengths: int32 [32], P(('rep', 'ep')), parts along dimension 0, may hold values from 2 to 1024, as said below
- uv_weight: bfloat16 [128, 512, 128], P('ep'), may hold values from -0.25 to 0.25
- out_weight: bfloat16 [128, 128, 7168], P('ep'), may hold values from -0.125 to 0.125
- moe_gain: float32 [7168], replicated, may hold values from 0.1 to 1.9
- route_ids: int32 [32, 1], P(('rep', 'ep')), parts along dimension 0, may hold values from 0 to 1
- route_scores: float32 [32, 1], P(('rep', 'ep')), parts along dimension 0, may hold values from 0.05 to 1
- expert_gate: bfloat16 [16, 7168, 128], P('ep'), may hold values from -0.0625 to 0.0625
- expert_up: bfloat16 [16, 7168, 128], P('ep'), may hold values from -0.0625 to 0.0625
- expert_down: bfloat16 [16, 128, 7168], P('ep'), may hold values from -0.1875 to 0.1875
Outputs:
- after_attention: bfloat16 [32, 7168], P(('rep', 'ep')), parts along dimension 0
- layer_out: bfloat16 [32, 7168], P(('rep', 'ep')), parts along dimension 0
The draws below stay inside these ranges and needn't reach their ends.
There are 2 independent parts, one for each index of `rep`. The reference program is written for one: setup_inputs(seed, part) draws one part's arguments, and reference() takes and returns one part's arrays. A program takes and returns all parts, laid end to end along the dimension named above; an argument that names none is the same for every part. Nothing has to cross between parts.
Inputs may be any that keep to these rules, and one draw needn't show every extreme that they name: `lengths`: every request has at least two cached positions; in every draw some request has exactly 1024.
All inputs are finite; a program needn't handle non-finite values.
Results may differ from the reference program's by a relative error of at most 0.008.
Values may be sent and summed in bfloat16 or wider, within the bound.
A program may use at most 128 MiB of HBM per device.

```python
import math
import jax
import jax.numpy as jnp
from jax import lax

D = 7168
H = 128
LAT = 512
ROPE = 64
HV = 128
FF = 9216
HE_DEV = 128
GROUP = 8
CACHE = 1024
ROWS = 16
EXPERTS = 2
TOP = 1
HE = 1024


def cache_base(key):
    dims = (ROWS, CACHE, LAT + ROPE)
    normal_part = jnp.clip(jax.random.normal(jax.random.fold_in(key, 1), dims, jnp.float32), -6.0, 6.0)
    values = normal_part
    first_key = values[:, 0:1, :]
    second_key = values[:, 1:2, :]
    return jnp.concatenate([first_key, second_key, values[:, 2:, :]], axis=1)


def draw_kv_cache(key, part):
    shared = cache_base(key)
    return shared.astype(jnp.bfloat16)


def draw_queries(key, part):
    key = jax.random.fold_in(key, 5)
    dims = (ROWS, H, LAT + ROPE)
    values = jnp.clip(jax.random.normal(key, dims, jnp.float32), -6.0, 6.0)
    return values.astype(jnp.bfloat16)


def draw_lengths(key, part):
    key = jax.random.fold_in(key, 7)
    drawn = jax.random.randint(jax.random.fold_in(key, 1), (ROWS,), 2, CACHE + 1)
    longest = jax.random.randint(jax.random.fold_in(key, 2), (), 0, ROWS)
    return jnp.where(jnp.arange(ROWS, dtype=jnp.int32) == longest, CACHE, drawn).astype(jnp.int32)


def draw_tokens(key, part):
    key = jax.random.fold_in(key, 9)
    row_scale = jnp.exp(jax.random.uniform(jax.random.fold_in(key, 1), (ROWS, 1), jnp.float32, 0.0, math.log(10.0)))
    column_scale = jnp.exp(jax.random.uniform(jax.random.fold_in(key, 2), (1, D), jnp.float32, 0.0, math.log(10.0)))
    values = jax.random.normal(jax.random.fold_in(key, 3), (ROWS, D), jnp.float32)
    return jnp.clip(values * row_scale * column_scale / 20.0, -3.0, 3.0).astype(jnp.bfloat16)


def levels(key, shape, shards, low, top_value):
    level, own = 1.0, jax.random.fold_in(key, 6)
    for dim, shards_of in shards:
        heights = jnp.exp(jax.random.uniform(jax.random.fold_in(own, dim), (shards_of,), jnp.float32, low / len(shards), top_value / len(shards)))
        level = level * jnp.repeat(heights, shape[dim] // shards_of).reshape([-1 if axis == dim else 1 for axis in range(len(shape))])
    return level


def distinct(own_key, rows, count, top, lift):
    sequence = jax.random.permutation(jax.random.fold_in(own_key, 1), count)
    pull = sequence
    for power in range(3):
        pull = pull * pull // count
    pull = pull * lift // count
    chance = jax.random.randint(jax.random.fold_in(own_key, 2), (rows, count), 0, 4096) + pull
    fixed_rows = jax.random.permutation(jax.random.fold_in(own_key, 3), rows)[jnp.arange(count) % rows]
    chance = jnp.where(jnp.arange(rows)[:, None] == fixed_rows[None, :], 1 << 14, chance)
    score = chance * count + jnp.arange(count)
    return lax.top_k(score.astype(jnp.int32), top)[1].astype(jnp.int32)


def bell_draw(own_key, shape, width, most, cuts=(), held_as=jnp.bfloat16):
    result = width * jax.random.normal(own_key, shape, jnp.float32)
    if cuts:
        result = result * levels(own_key, shape, cuts, -0.22, 0.18)
    return jnp.clip(result, -most, most).astype(held_as)


def setup_inputs(seed: int = 0, part: int = 0) -> dict:
    key_list = jax.random.split(jax.random.key(seed), 18)
    part_splits = jax.random.split(jax.random.fold_in(key_list[17], part), 18)
    return {
        "tokens": draw_tokens(jax.random.fold_in(jax.random.fold_in(key_list[17], part), 71), part),
        "ffn_gain": jnp.clip(1.0 + 0.18 * jax.random.normal(key_list[1], (D,), jnp.float32), 0.1, 1.9),
        "gate_weight": bell_draw(key_list[2], (D, FF), D ** -0.5, 0.0625, ((1, 16),)),
        "up_weight": bell_draw(key_list[3], (D, FF), D ** -0.5, 0.0625, ((1, 16),)),
        "down_weight": bell_draw(key_list[4], (FF, D), FF ** -0.5, 0.0625, ((0, 16),)),
        "queries": draw_queries(jax.random.fold_in(jax.random.fold_in(key_list[17], part), 71), part),
        "kv_cache": draw_kv_cache(jax.random.fold_in(jax.random.fold_in(key_list[17], part), 71), part),
        "new_kv": bell_draw(part_splits[7], (ROWS, LAT + ROPE), 1.0, 6.0, ((0, 16),)),
        "lengths": draw_lengths(jax.random.fold_in(jax.random.fold_in(key_list[17], part), 71), part),
        "uv_weight": bell_draw(key_list[9], (H, LAT, HV), LAT ** -0.5, 0.25, ((0, 16),)),
        "out_weight": bell_draw(key_list[10], (H, HV, D), (HV * 16) ** -0.5, 0.125, ((0, 16),)),
        "moe_gain": jnp.clip(1.0 + 0.18 * jax.random.normal(key_list[11], (D,), jnp.float32), 0.1, 1.9),
        "route_ids": distinct(part_splits[12], ROWS, EXPERTS, TOP, 8192),
        "route_scores": jnp.clip(jnp.exp(math.log(1.0) - 2.9957323 * jax.random.uniform(part_splits[13], (ROWS, TOP), jnp.float32) ** levels(part_splits[13], (ROWS, TOP), ((0, 16),), -0.2, 0.2)), 0.05, 1.0),
        "expert_gate": bell_draw(key_list[14], (EXPERTS * GROUP, D, HE_DEV), D ** -0.5, 0.0625, ((0, 16),)),
        "expert_up": bell_draw(key_list[15], (EXPERTS * GROUP, D, HE_DEV), D ** -0.5, 0.0625, ((0, 16),)),
        "expert_down": bell_draw(key_list[16], (EXPERTS * GROUP, HE_DEV, D), HE ** -0.5, 0.1875, ((0, 16),)),
    }


def rms_norm(matrix, gain):
    values = matrix.astype(jnp.float32)
    mean_square = lax.optimization_barrier(jnp.mean(values * values, axis=-1, keepdims=True))
    return values * lax.rsqrt(mean_square + 1e-06) * gain.astype(jnp.float32)

def attend_request(pieces):
    query_rows, cache_rows, fresh_key, length = pieces
    factor = (HV + ROPE) ** (-0.5)
    scores = jnp.dot(query_rows, cache_rows.T, preferred_element_type=jnp.float32) * factor
    positions = jnp.arange(cache_rows.shape[0], dtype=jnp.int32)
    usable = positions[None, :] < length
    own_score = jnp.dot(query_rows, fresh_key, preferred_element_type=jnp.float32) * factor
    highest = jnp.maximum(lax.optimization_barrier(jnp.max(jnp.where(usable, scores, -jnp.inf), axis=1)), own_score)
    weights = jnp.where(usable, jnp.exp(scores - highest[:, None]), 0.0)
    own_weight = jnp.exp(own_score - highest)
    totals = lax.optimization_barrier(jnp.sum(weights, axis=1)) + own_weight
    probs_cache = (weights / totals[:, None]).astype(jnp.bfloat16)
    probs_own = (own_weight / totals).astype(jnp.bfloat16)
    context = jnp.dot(probs_cache, cache_rows[:, :LAT], preferred_element_type=jnp.float32)
    context = context + probs_own.astype(jnp.float32)[:, None] * fresh_key[:LAT].astype(jnp.float32)[None, :]
    return context.astype(jnp.bfloat16)

def reference(tokens, ffn_gain, gate_weight, up_weight, down_weight, queries, kv_cache, new_kv, lengths, uv_weight, out_weight, moe_gain, route_ids, route_scores, expert_gate, expert_up, expert_down):
    normed = rms_norm(tokens, ffn_gain).astype(jnp.bfloat16)
    gate_values = jnp.dot(normed, gate_weight, preferred_element_type=jnp.float32)
    up_values = jnp.dot(normed, up_weight, preferred_element_type=jnp.float32)
    ffn_hidden = (jax.nn.silu(gate_values) * up_values).astype(jnp.bfloat16)
    ffn_out = jnp.dot(ffn_hidden, down_weight, preferred_element_type=jnp.float32)
    context = lax.map(attend_request, (queries, kv_cache, new_kv, lengths))
    head_out = jnp.einsum('rhl,hlv->rhv', context.astype(jnp.float32), uv_weight.astype(jnp.float32)).astype(jnp.bfloat16)
    attention_out = jnp.dot(head_out.reshape(ROWS, H * HV), out_weight.reshape(H * HV, D), preferred_element_type=jnp.float32)
    after_attention = (tokens.astype(jnp.float32) + (ffn_out + attention_out)).astype(jnp.bfloat16)
    moe_in = rms_norm(after_attention, moe_gain).astype(jnp.bfloat16)
    combine = (2.5 / TOP * route_scores).astype(jnp.bfloat16)
    matches = route_ids[:, :, None] == jnp.arange(EXPERTS, dtype=jnp.int32)[None, None, :]
    table = lax.optimization_barrier(jnp.sum(jnp.where(matches, combine.astype(jnp.float32)[:, :, None], 0.0), axis=1))
    gate_blocks = expert_gate.reshape(EXPERTS, GROUP, D, HE_DEV)
    up_blocks = expert_up.reshape(EXPERTS, GROUP, D, HE_DEV)
    down_blocks = expert_down.reshape(EXPERTS, GROUP, HE_DEV, D)

    def add_expert(running, pieces):
        gate_block, up_block, down_block, column = pieces
        gate_full = jnp.transpose(gate_block, (1, 0, 2)).reshape(D, GROUP * HE_DEV)
        up_full = jnp.transpose(up_block, (1, 0, 2)).reshape(D, GROUP * HE_DEV)
        down_full = down_block.reshape(GROUP * HE_DEV, D)
        gate_part = jnp.dot(moe_in, gate_full, preferred_element_type=jnp.float32)
        up_part = jnp.dot(moe_in, up_full, preferred_element_type=jnp.float32)
        hidden = (jax.nn.silu(gate_part) * up_part).astype(jnp.bfloat16)
        expert_out = jnp.dot(hidden, down_full, preferred_element_type=jnp.float32)
        return (running + column[:, None] * expert_out, None)
    moe_out, _ = lax.scan(add_expert, jnp.zeros((ROWS, D), jnp.float32), (gate_blocks, up_blocks, down_blocks, jnp.transpose(table)))
    layer_out = (after_attention.astype(jnp.float32) + moe_out).astype(jnp.bfloat16)
    return (after_attention, layer_out)
```

```python
import functools

import jax
import jax.numpy as jnp
from jax import lax
from jax.experimental import pallas as pl
from jax.experimental.pallas import tpu as pltpu
from jax.sharding import PartitionSpec as P

LAT = 512
ROPE = 64
HV = 128
GROUP = 8
W = 512
F32 = jnp.float32
BF16 = jnp.bfloat16
MESH = pl.DeviceIdType.MESH


def dot(a, b):
    return jnp.dot(a, b, preferred_element_type=F32)


def silu(v):
    return v / (1.0 + jnp.exp(-v))


class Exchange:
    def __init__(self, n, me, src, dst, send_sem, recv_sem):
        self.n, self.me, self.src, self.dst = n, me, src, dst
        self.send_sem, self.recv_sem = send_sem, recv_sem

    def copy(self, d, slot):
        peer = lax.rem(self.me + d, self.n)
        return pltpu.make_async_remote_copy(
            src_ref=self.src(peer),
            dst_ref=self.dst.at[slot],
            send_sem=self.send_sem.at[d],
            recv_sem=self.recv_sem.at[d],
            device_id={"ep": peer},
            device_id_type=MESH,
        )

    def start(self):
        @pl.loop(1, self.n)
        def _(d):
            self.copy(d, self.me).start()

    def wait_recv(self):
        @pl.loop(1, self.n)
        def _(d):
            self.copy(d, lax.rem(self.me - d + self.n, self.n)).wait_recv()

    def wait_send(self):
        @pl.loop(1, self.n)
        def _(d):
            self.copy(d, self.me).wait_send()


def kernel(
    n, hpd, tok_ref, gain_ref, nkv_ref, len_ref, gain2_ref, ids_ref, score_ref,
    q_hbm, kv_hbm, gate_hbm, up_hbm, uv_hbm, out_hbm, down_hbm, eg_hbm, eu_hbm, ed_hbm,
    after_ref, layer_ref,
    q, kv, gate, up, uv, out, down, eg, eu, ed,
    row_f32, gain_rows, send1, recv1, ctx_send, ctx_recv, rs1_send, rs1_recv,
    send2, recv2, rs2_send, rs2_recv, wide, lhs, flat,
    load_sem, ssem, rsem,
):
    width = tok_ref.shape[1]
    chunks = width // W
    me = lax.axis_index("ep")
    barrier = pltpu.get_barrier_semaphore()

    @pl.loop(1, n)
    def _(d):
        pl.semaphore_signal(
            barrier, inc=1, device_id={"ep": lax.rem(me + d, n)}, device_id_type=MESH
        )

    loads = [
        pltpu.make_async_copy(src, dst, load_sem.at[i])
        for i, (src, dst) in enumerate(
            [(q_hbm, q), (kv_hbm, kv), (gate_hbm, gate), (up_hbm, up), (uv_hbm, uv),
             (out_hbm, out), (down_hbm, down), (eg_hbm, eg), (eu_hbm, eu), (ed_hbm, ed)]
        )
    ]
    for load in loads:
        load.start()
    (q_in, kv_in, gate_in, up_in, uv_in, out_in, down_in, eg_in, eu_in, ed_in) = loads

    def fold(src, dst):
        dst[...] = jnp.zeros_like(dst)
        for c in range(chunks):
            dst[c : c + 1, :] = src[0:1, c * W : (c + 1) * W].astype(F32)

    def norm(values, gain):
        squares = jnp.sum(jnp.sum(values * values, axis=1, keepdims=True), axis=0, keepdims=True)
        return values * lax.rsqrt(squares / width + 1e-06) * gain

    def unfold_rows(buffer):
        wide[...] = buffer[...].astype(F32)
        for c in range(chunks):
            lhs[c] = wide[:, c, :].astype(BF16)

    def total(buffer):
        def step(i, acc):
            return acc + buffer[i].astype(F32)

        return lax.fori_loop(0, n, step, jnp.zeros((16, W), F32), unroll=4)

    rows = lax.broadcasted_iota(jnp.int32, (16, W), 0)
    lanes = lax.broadcasted_iota(jnp.int32, (16, W), 1)

    fold(tok_ref, row_f32)
    fold(gain_ref, gain_rows)
    send1[...] = norm(row_f32[...], gain_rows[...]).astype(BF16)
    gather1 = Exchange(n, me, lambda peer: send1, recv1, ssem.at[0], rsem.at[0])
    recv1[me] = send1[...]
    pl.semaphore_wait(barrier, n - 1)
    gather1.start()

    q_in.wait()
    kv_in.wait()
    factor = (HV + ROPE) ** (-0.5)
    keys = kv[...]
    queries = q[...]
    scores = (
        lax.dot_general(queries, keys, (((1,), (1,)), ((), ())), preferred_element_type=F32)
        * factor
    )
    fresh = nkv_ref[...].astype(F32)
    own = jnp.sum(queries.astype(F32) * fresh, axis=1, keepdims=True) * factor
    usable = lax.broadcasted_iota(jnp.int32, scores.shape, 1) < len_ref[...]
    highest = jnp.maximum(
        jnp.max(jnp.where(usable, scores, -jnp.inf), axis=1, keepdims=True), own
    )
    weights = jnp.where(usable, jnp.exp(scores - highest), 0.0)
    own_weight = jnp.exp(own - highest)
    totals = jnp.sum(weights, axis=1, keepdims=True) + own_weight
    probs = (weights / totals).astype(BF16)
    probs_own = (own_weight / totals).astype(BF16).astype(F32)
    context = dot(probs, kv[:, :LAT]) + probs_own * fresh[:, :LAT]
    ctx_send[...] = context.astype(BF16).astype(F32).reshape(ctx_send.shape)
    ctx_recv[me] = ctx_send[me]
    spread = Exchange(n, me, lambda peer: ctx_send.at[peer], ctx_recv, ssem.at[1], rsem.at[1])
    spread.start()

    gather1.wait_recv()
    unfold_rows(recv1)
    gate_in.wait()
    up_in.wait()
    gate_part = jnp.zeros((n, gate.shape[1]), F32)
    up_part = jnp.zeros((n, up.shape[1]), F32)
    for c in range(chunks):
        part = slice(c * W, (c + 1) * W)
        gate_part += dot(lhs[c], gate[part, :])
        up_part += dot(lhs[c], up[part, :])
    hidden = (silu(gate_part) * up_part).astype(BF16)

    spread.wait_recv()
    uv_in.wait()
    for h in range(hpd):
        flat[:, h * HV : (h + 1) * HV] = dot(ctx_recv[:, h, :].astype(BF16), uv[h]).astype(BF16)
    out_in.wait()
    down_in.wait()
    heads = flat[...]
    for c in range(chunks):
        part = slice(c * W, (c + 1) * W)
        wide[:, c, :] = dot(hidden, down[:, part]) + dot(heads, out[:, part])
    rs1_send[...] = wide[...].astype(BF16)
    rs1_recv[me] = rs1_send[me]
    sum1 = Exchange(n, me, lambda peer: rs1_send.at[peer], rs1_recv, ssem.at[2], rsem.at[2])
    sum1.start()
    fold(gain2_ref, gain_rows)
    combine = (2.5 / ids_ref.shape[1] * score_ref[...]).astype(BF16).astype(F32)
    table = jnp.zeros((16, W), F32)
    for k in range(ids_ref.shape[1]):
        table += jnp.where(lanes == ids_ref[0:1, k : k + 1], combine[0:1, k : k + 1], 0.0)
    sum1.wait_recv()
    after = jnp.where(rows < chunks, row_f32[...] + total(rs1_recv), 0.0).astype(BF16).astype(F32)
    for c in range(chunks):
        after_ref[0:1, c * W : (c + 1) * W] = after[c : c + 1, :].astype(BF16)
    row_f32[...] = after

    moe_in = norm(after, gain_rows[...])
    send2[...] = jnp.where(rows == chunks, table, moe_in).astype(BF16)
    recv2[me] = send2[...]
    gather2 = Exchange(n, me, lambda peer: send2, recv2, ssem.at[3], rsem.at[3])
    gather2.start()
    eg_in.wait()
    eu_in.wait()
    ed_in.wait()
    gather2.wait_recv()
    unfold_rows(recv2)
    columns = wide[:, chunks, :]
    mine = lax.broadcasted_iota(jnp.int32, columns.shape, 1) == me // GROUP
    column = jnp.sum(jnp.where(mine, columns, 0.0), axis=1, keepdims=True)
    gate_part = jnp.zeros((n, eg.shape[1]), F32)
    up_part = jnp.zeros((n, eu.shape[1]), F32)
    for c in range(chunks):
        part = slice(c * W, (c + 1) * W)
        gate_part += dot(lhs[c], eg[part, :])
        up_part += dot(lhs[c], eu[part, :])
    expert_hidden = (silu(gate_part) * up_part).astype(BF16)
    for c in range(chunks):
        wide[:, c, :] = dot(expert_hidden, ed[:, c * W : (c + 1) * W]) * column
    rs2_send[...] = wide[...].astype(BF16)
    rs2_recv[me] = rs2_send[me]
    sum2 = Exchange(n, me, lambda peer: rs2_send.at[peer], rs2_recv, ssem.at[4], rsem.at[4])
    sum2.start()
    gather1.wait_send()
    spread.wait_send()
    sum1.wait_send()
    gather2.wait_send()
    sum2.wait_recv()
    layer = row_f32[...] + total(rs2_recv)
    for c in range(chunks):
        layer_ref[0:1, c * W : (c + 1) * W] = layer[c : c + 1, :].astype(BF16)
    sum2.wait_send()


def body(
    tokens, ffn_gain, gate_weight, up_weight, down_weight, queries, kv_cache, new_kv, lengths,
    uv_weight, out_weight, moe_gain, route_ids, route_scores, expert_gate, expert_up, expert_down,
):
    n = lax.axis_size("ep")
    width = tokens.shape[1]
    hpd = uv_weight.shape[0]
    chunks = width // W
    assert tokens.shape[0] == 1 and width % W == 0 and chunks < 16
    big = (
        queries[0], kv_cache[0], gate_weight, up_weight, uv_weight,
        out_weight.reshape(-1, width), down_weight,
        expert_gate[0], expert_up[0], expert_down[0],
    )
    vmem = pl.BlockSpec(memory_space=pltpu.VMEM)
    slots = pltpu.VMEM((n, 16, W), BF16)
    return pl.pallas_call(
        functools.partial(kernel, n, hpd),
        out_shape=[jax.ShapeDtypeStruct((1, width), BF16)] * 2,
        in_specs=[vmem] * 7 + [pl.BlockSpec(memory_space=pl.ANY)] * len(big),
        out_specs=[vmem] * 2,
        scratch_shapes=[pltpu.VMEM(x.shape, x.dtype) for x in big]
        + [
            pltpu.VMEM((16, W), F32),
            pltpu.VMEM((16, W), F32),
            pltpu.VMEM((16, W), BF16),
            slots,
            pltpu.VMEM((n, hpd, LAT), F32),
            pltpu.VMEM((n, hpd, LAT), F32),
            slots,
            slots,
            pltpu.VMEM((16, W), BF16),
            slots,
            slots,
            slots,
            pltpu.VMEM((n, 16, W), F32),
            pltpu.VMEM((chunks, n, W), BF16),
            pltpu.VMEM((n, hpd * HV), BF16),
            pltpu.SemaphoreType.DMA((len(big),)),
            pltpu.SemaphoreType.DMA((5, n)),
            pltpu.SemaphoreType.DMA((5, n)),
        ],
        compiler_params=pltpu.CompilerParams(
            collective_id=0, has_side_effects=True, vmem_limit_bytes=60 * 1024 * 1024
        ),
    )(
        tokens, ffn_gain.reshape(1, width), new_kv, lengths.reshape(1, 1),
        moe_gain.reshape(1, width), route_ids, route_scores, *big,
    )


def solution(mesh):
    in_specs = (
        P(("rep", "ep"), None),
        P(),
        P(None, "ep"),
        P(None, "ep"),
        P("ep", None),
        P(("rep", "ep"), None, None),
        P(("rep", "ep"), None, None),
        P(("rep", "ep"), None),
        P(("rep", "ep")),
        P("ep", None, None),
        P("ep", None, None),
        P(),
        P(("rep", "ep"), None),
        P(("rep", "ep"), None),
        P("ep", None, None),
        P("ep", None, None),
        P("ep", None, None),
    )
    out_specs = (P(("rep", "ep"), None), P(("rep", "ep"), None))
    return jax.shard_map(body, mesh=mesh, in_specs=in_specs, out_specs=out_specs, check_vma=False)
```

```python
import functools

import jax
import jax.numpy as jnp
from jax import lax
from jax.experimental import pallas as pl
from jax.experimental.pallas import tpu as pltpu
from jax.sharding import PartitionSpec as P

LAT = 512
ROPE = 64
HV = 128
GROUP = 8
W = 256
F32 = jnp.float32
BF16 = jnp.bfloat16
MESH = pl.DeviceIdType.MESH


def dot(a, b):
    return jnp.dot(a, b, preferred_element_type=F32)


def dot_nt(a, b):
    return lax.dot_general(a, b, (((1,), (1,)), ((), ())), preferred_element_type=F32)


def silu(v):
    return v / (1.0 + jnp.exp(-v))


class Exchange:
    def __init__(self, n, me, src, dst, send_sem, recv_sem):
        self.n, self.me, self.src, self.dst = n, me, src, dst
        self.send_sem, self.recv_sem = send_sem, recv_sem

    def copy(self, d, slot):
        peer = lax.rem(self.me + d, self.n)
        return pltpu.make_async_remote_copy(
            src_ref=self.src(peer),
            dst_ref=self.dst.at[slot],
            send_sem=self.send_sem.at[d],
            recv_sem=self.recv_sem.at[d],
            device_id={"ep": peer},
            device_id_type=MESH,
        )

    def start(self):
        @pl.loop(1, self.n)
        def _(d):
            self.copy(d, self.me).start()

    def wait_recv(self):
        @pl.loop(1, self.n)
        def _(d):
            self.copy(d, lax.rem(self.me - d + self.n, self.n)).wait_recv()

    def wait_send(self):
        @pl.loop(1, self.n)
        def _(d):
            self.copy(d, self.me).wait_send()


def kernel(
    n, hpd, tok_ref, gain_ref, nkv_ref, len_ref, gain2_ref, ids_ref, score_ref,
    q_hbm, kv_hbm, gate_hbm, up_hbm, uv_hbm, out_hbm, down_hbm, eg_hbm, eu_hbm, ed_hbm,
    after_ref, layer_ref,
    q, kv, gate, up, uv, out, down, eg, eu, ed,
    row_f32, gain_rows, send1, recv1, ctx_send, ctx_recv, rs1_send, rs1_recv,
    send2, recv2, rs2_send, rs2_recv, wide, narrow, lhs, flat,
    load_sem, ssem, rsem,
):
    width = tok_ref.shape[1]
    chunks = width // (2 * W)
    half = width // 2
    me = lax.axis_index("ep")
    barrier = pltpu.get_barrier_semaphore()

    @pl.loop(1, n)
    def _(d):
        pl.semaphore_signal(
            barrier, inc=1, device_id={"ep": lax.rem(me + d, n)}, device_id_type=MESH
        )

    jobs = [(q_hbm, q, None), (kv_hbm, kv, None)]
    jobs += [(src, dst, hf) for hf in (0, 1) for src, dst in ((gate_hbm, gate), (up_hbm, up))]
    jobs += [(uv_hbm, uv, None)]
    jobs += [(src, dst, hf) for hf in (0, 1) for src, dst in ((out_hbm, out), (down_hbm, down))]
    jobs += [(eg_hbm, eg, None), (eu_hbm, eu, None), (ed_hbm, ed, None)]
    loads = []
    for i, (src, dst, hf) in enumerate(jobs):
        if hf is not None:
            src, dst = (ref.at[:, pl.ds(hf * half, half)] for ref in (src, dst))
        loads.append(pltpu.make_async_copy(src, dst, load_sem.at[i]))
        loads[-1].start()
    (q_in, kv_in, gate_a, up_a, gate_b, up_b, uv_in, out_a, down_a, out_b, down_b,
     eg_in, eu_in, ed_in) = loads
    projections = ((gate_a, up_a), (gate_b, up_b))
    branches = ((out_a, down_a), (out_b, down_b))

    def fold(src, dst):
        dst[...] = jnp.zeros_like(dst)
        for j in range(2 * chunks):
            hf, c = divmod(j, chunks)
            dst[c : c + 1, hf * W : (hf + 1) * W] = src[0:1, j * W : (j + 1) * W].astype(F32)

    def unfold(values, dst):
        for j in range(2 * chunks):
            hf, c = divmod(j, chunks)
            dst[0:1, j * W : (j + 1) * W] = values[c : c + 1, hf * W : (hf + 1) * W].astype(BF16)

    def norm(values, gain):
        squares = jnp.sum(jnp.sum(values * values, axis=1, keepdims=True), axis=0, keepdims=True)
        return values * lax.rsqrt(squares / width + 1e-06) * gain

    def unfold_rows(buffer):
        wide[...] = buffer[...].astype(F32)
        for j in range(2 * chunks):
            hf, c = divmod(j, chunks)
            lhs[j] = wide[:, c, hf * W : (hf + 1) * W].astype(BF16)

    def total(buffer, hf):
        def step(i, acc):
            return acc + buffer[hf, i].astype(F32)

        return lax.fori_loop(0, n, step, jnp.zeros((16, W), F32), unroll=4)

    def scatter(send, recv, hf, sem):
        send[hf] = narrow[...].astype(BF16)
        recv[hf, me] = send[hf, me]
        exchange = Exchange(
            n, me, lambda peer: send.at[hf, peer], recv.at[hf], ssem.at[sem], rsem.at[sem]
        )
        exchange.start()
        return exchange

    narrow[...] = jnp.zeros_like(narrow)
    rows = lax.broadcasted_iota(jnp.int32, (16, 2 * W), 0)
    lanes = lax.broadcasted_iota(jnp.int32, (16, 2 * W), 1)

    fold(tok_ref, row_f32)
    fold(gain_ref, gain_rows)
    send1[...] = norm(row_f32[...], gain_rows[...]).astype(BF16)
    gather1 = Exchange(n, me, lambda peer: send1, recv1, ssem.at[0], rsem.at[0])
    recv1[me] = send1[...]
    pl.semaphore_wait(barrier, n - 1)
    gather1.start()

    q_in.wait()
    kv_in.wait()
    factor = (HV + ROPE) ** (-0.5)
    queries = q[...].astype(F32).T
    scores = dot(queries.astype(BF16), kv[...]) * factor
    fresh = nkv_ref[...].astype(F32)
    own = jnp.sum(queries * fresh, axis=1, keepdims=True) * factor
    usable = lax.broadcasted_iota(jnp.int32, scores.shape, 1) < len_ref[...]
    highest = jnp.maximum(
        jnp.max(jnp.where(usable, scores, -jnp.inf), axis=1, keepdims=True), own
    )
    weights = jnp.where(usable, jnp.exp(scores - highest), 0.0)
    own_weight = jnp.exp(own - highest)
    totals = jnp.sum(weights, axis=1, keepdims=True) + own_weight
    probs = (weights / totals).astype(BF16)
    probs_own = (own_weight / totals).astype(BF16).astype(F32)
    context = dot_nt(probs, kv[:LAT, :]) + probs_own * fresh[:, :LAT]
    ctx_send[...] = context.astype(BF16).astype(F32).reshape(ctx_send.shape)
    ctx_recv[me] = ctx_send[me]
    spread = Exchange(n, me, lambda peer: ctx_send.at[peer], ctx_recv, ssem.at[1], rsem.at[1])
    spread.start()

    gather1.wait_recv()
    unfold_rows(recv1)
    gate_part = jnp.zeros((n, gate.shape[0]), F32)
    up_part = jnp.zeros((n, up.shape[0]), F32)
    for j in range(2 * chunks):
        if j % chunks == 0:
            for load in projections[j // chunks]:
                load.wait()
        part = slice(j * W, (j + 1) * W)
        gate_part += dot_nt(lhs[j], gate[:, part])
        up_part += dot_nt(lhs[j], up[:, part])
    hidden = (silu(gate_part) * up_part).astype(BF16)

    spread.wait_recv()
    uv_in.wait()
    for h in range(hpd):
        flat[:, h * HV : (h + 1) * HV] = dot(ctx_recv[:, h, :].astype(BF16), uv[h]).astype(BF16)
    heads = flat[...]
    sum1 = []
    for hf in (0, 1):
        for load in branches[hf]:
            load.wait()
        for c in range(chunks):
            part = slice(hf * half + c * W, hf * half + (c + 1) * W)
            narrow[:, c, :] = dot(hidden, down[:, part]) + dot(heads, out[:, part])
        sum1.append(scatter(rs1_send, rs1_recv, hf, 2 + hf))
    fold(gain2_ref, gain_rows)
    combine = (2.5 / ids_ref.shape[1] * score_ref[...]).astype(BF16).astype(F32)
    table = jnp.zeros((16, 2 * W), F32)
    for k in range(ids_ref.shape[1]):
        table += jnp.where(lanes == ids_ref[0:1, k : k + 1], combine[0:1, k : k + 1], 0.0)
    sums = []
    for hf in (0, 1):
        sum1[hf].wait_recv()
        sums.append(total(rs1_recv, hf))
    after = row_f32[...] + jnp.concatenate(sums, axis=1)
    after = jnp.where(rows < chunks, after, 0.0).astype(BF16).astype(F32)
    unfold(after, after_ref)
    row_f32[...] = after

    moe_in = norm(after, gain_rows[...])
    send2[...] = jnp.where(rows == chunks, table, moe_in).astype(BF16)
    recv2[me] = send2[...]
    gather2 = Exchange(n, me, lambda peer: send2, recv2, ssem.at[4], rsem.at[4])
    gather2.start()
    eg_in.wait()
    eu_in.wait()
    ed_in.wait()
    gather2.wait_recv()
    unfold_rows(recv2)
    columns = wide[:, chunks, :]
    mine = lax.broadcasted_iota(jnp.int32, columns.shape, 1) == me // GROUP
    column = jnp.sum(jnp.where(mine, columns, 0.0), axis=1, keepdims=True)
    gate_part = jnp.zeros((n, eg.shape[1]), F32)
    up_part = jnp.zeros((n, eu.shape[1]), F32)
    for j in range(2 * chunks):
        part = slice(j * W, (j + 1) * W)
        gate_part += dot(lhs[j], eg[part, :])
        up_part += dot(lhs[j], eu[part, :])
    expert_hidden = (silu(gate_part) * up_part).astype(BF16)
    sum2 = []
    for hf in (0, 1):
        for c in range(chunks):
            part = slice(hf * half + c * W, hf * half + (c + 1) * W)
            narrow[:, c, :] = dot(expert_hidden, ed[:, part]) * column
        sum2.append(scatter(rs2_send, rs2_recv, hf, 5 + hf))
    for exchange in (gather1, spread, *sum1, gather2):
        exchange.wait_send()
    sums = []
    for hf in (0, 1):
        sum2[hf].wait_recv()
        sums.append(total(rs2_recv, hf))
    layer = row_f32[...] + jnp.concatenate(sums, axis=1)
    unfold(layer, layer_ref)
    for exchange in sum2:
        exchange.wait_send()


def body(
    tokens, ffn_gain, gate_weight, up_weight, down_weight, queries, kv_cache, new_kv, lengths,
    uv_weight, out_weight, moe_gain, route_ids, route_scores, expert_gate, expert_up, expert_down,
):
    n = lax.axis_size("ep")
    width = tokens.shape[1]
    hpd = uv_weight.shape[0]
    chunks = width // (2 * W)
    assert tokens.shape[0] == 1 and width % (2 * W) == 0 and chunks < 16
    big = (
        queries[0].T, kv_cache[0].T, gate_weight.T, up_weight.T, uv_weight,
        out_weight.reshape(-1, width), down_weight,
        expert_gate[0], expert_up[0], expert_down[0],
    )
    vmem = pl.BlockSpec(memory_space=pltpu.VMEM)
    slots = pltpu.VMEM((n, 16, 2 * W), BF16)
    halves = pltpu.VMEM((2, n, 16, W), BF16)
    return pl.pallas_call(
        functools.partial(kernel, n, hpd),
        out_shape=[jax.ShapeDtypeStruct((1, width), BF16)] * 2,
        in_specs=[vmem] * 7 + [pl.BlockSpec(memory_space=pl.ANY)] * len(big),
        out_specs=[vmem] * 2,
        scratch_shapes=[pltpu.VMEM(x.shape, x.dtype) for x in big]
        + [
            pltpu.VMEM((16, 2 * W), F32),
            pltpu.VMEM((16, 2 * W), F32),
            pltpu.VMEM((16, 2 * W), BF16),
            slots,
            pltpu.VMEM((n, hpd, LAT), F32),
            pltpu.VMEM((n, hpd, LAT), F32),
            halves,
            halves,
            pltpu.VMEM((16, 2 * W), BF16),
            slots,
            halves,
            halves,
            pltpu.VMEM((n, 16, 2 * W), F32),
            pltpu.VMEM((n, 16, W), F32),
            pltpu.VMEM((2 * chunks, n, W), BF16),
            pltpu.VMEM((n, hpd * HV), BF16),
            pltpu.SemaphoreType.DMA((len(big) + 4,)),
            pltpu.SemaphoreType.DMA((7, n)),
            pltpu.SemaphoreType.DMA((7, n)),
        ],
        compiler_params=pltpu.CompilerParams(
            collective_id=0, has_side_effects=True, vmem_limit_bytes=60 * 1024 * 1024
        ),
    )(
        tokens, ffn_gain.reshape(1, width), new_kv, lengths.reshape(1, 1),
        moe_gain.reshape(1, width), route_ids, route_scores, *big,
    )


def solution(mesh):
    in_specs = (
        P(("rep", "ep"), None),
        P(),
        P(None, "ep"),
        P(None, "ep"),
        P("ep", None),
        P(("rep", "ep"), None, None),
        P(("rep", "ep"), None, None),
        P(("rep", "ep"), None),
        P(("rep", "ep")),
        P("ep", None, None),
        P("ep", None, None),
        P(),
        P(("rep", "ep"), None),
        P(("rep", "ep"), None),
        P("ep", None, None),
        P("ep", None, None),
        P("ep", None, None),
    )
    out_specs = (P(("rep", "ep"), None), P(("rep", "ep"), None))
    return jax.shard_map(body, mesh=mesh, in_specs=in_specs, out_specs=out_specs, check_vma=False)
```

```python
import functools

import jax
import jax.numpy as jnp
from jax import lax
from jax.experimental import pallas as pl
from jax.experimental.pallas import tpu as pltpu
from jax.sharding import PartitionSpec as P

LAT = 512
ROPE = 64
HV = 128
GROUP = 8
W = 256
F32 = jnp.float32
BF16 = jnp.bfloat16
MESH = pl.DeviceIdType.MESH


def dot(a, b):
    return jnp.dot(a, b, preferred_element_type=F32)


def dot_nt(a, b):
    return lax.dot_general(a, b, (((1,), (1,)), ((), ())), preferred_element_type=F32)


def silu(v):
    return v / (1.0 + jnp.exp(-v))


class Exchange:
    def __init__(self, n, me, src, dst, send_sem, recv_sem):
        self.n, self.me, self.src, self.dst = n, me, src, dst
        self.send_sem, self.recv_sem = send_sem, recv_sem

    def copy(self, d, slot):
        peer = lax.rem(self.me + d, self.n)
        return pltpu.make_async_remote_copy(
            src_ref=self.src(peer),
            dst_ref=self.dst.at[slot],
            send_sem=self.send_sem.at[d],
            recv_sem=self.recv_sem.at[d],
            device_id={"ep": peer},
            device_id_type=MESH,
        )

    def start(self):
        @pl.loop(1, self.n)
        def _(d):
            self.copy(d, self.me).start()

    def wait_recv(self):
        @pl.loop(1, self.n)
        def _(d):
            self.copy(d, lax.rem(self.me - d + self.n, self.n)).wait_recv()

    def wait_send(self):
        @pl.loop(1, self.n)
        def _(d):
            self.copy(d, self.me).wait_send()


def kernel(
    n, hpd, tok_ref, gain_ref, nkv_ref, len_ref, gain2_ref, ids_ref, score_ref,
    q_hbm, kv_hbm, gate_hbm, up_hbm, uv_hbm, out_hbm, down_hbm, eg_hbm, eu_hbm, ed_hbm,
    after_ref, layer_ref,
    q, kv, gate, up, uv, out, down, eg, eu, ed,
    row_f32, gain_rows, send1, recv1, ctx_send, ctx_recv, rs1_send, rs1_recv,
    send2, recv2, rs2_send, rs2_recv, wide, lhs, flat,
    load_sem, ssem, rsem,
):
    width = tok_ref.shape[1]
    chunks = width // (2 * W)
    half = width // 2
    me = lax.axis_index("ep")
    barrier = pltpu.get_barrier_semaphore()

    @pl.loop(1, n)
    def _(d):
        pl.semaphore_signal(
            barrier, inc=1, device_id={"ep": lax.rem(me + d, n)}, device_id_type=MESH
        )

    jobs = [(q_hbm, q, None), (kv_hbm, kv, None)]
    jobs += [(src, dst, hf) for hf in (0, 1) for src, dst in ((gate_hbm, gate), (up_hbm, up))]
    jobs += [(uv_hbm, uv, None)]
    jobs += [(src, dst, hf) for hf in (0, 1) for src, dst in ((out_hbm, out), (down_hbm, down))]
    jobs += [(eg_hbm, eg, None), (eu_hbm, eu, None), (ed_hbm, ed, None)]
    loads = []
    for i, (src, dst, hf) in enumerate(jobs):
        if hf is not None:
            src, dst = (ref.at[:, pl.ds(hf * half, half)] for ref in (src, dst))
        loads.append(pltpu.make_async_copy(src, dst, load_sem.at[i]))
        loads[-1].start()
    (q_in, kv_in, gate_a, up_a, gate_b, up_b, uv_in, out_a, down_a, out_b, down_b,
     eg_in, eu_in, ed_in) = loads
    projections = ((gate_a, up_a), (gate_b, up_b))
    branches = ((out_a, down_a), (out_b, down_b))

    def fold(src, dst):
        dst[...] = jnp.zeros_like(dst)
        for j in range(2 * chunks):
            hf, c = divmod(j, chunks)
            dst[c : c + 1, hf * W : (hf + 1) * W] = src[0:1, j * W : (j + 1) * W].astype(F32)

    def unfold(values, dst):
        for j in range(2 * chunks):
            hf, c = divmod(j, chunks)
            dst[0:1, j * W : (j + 1) * W] = values[c : c + 1, hf * W : (hf + 1) * W].astype(BF16)

    def norm(values, gain):
        squares = jnp.sum(jnp.sum(values * values, axis=1, keepdims=True), axis=0, keepdims=True)
        return values * lax.rsqrt(squares / width + 1e-06) * gain

    def unfold_rows(buffer):
        wide[...] = buffer[...].astype(F32)
        for j in range(2 * chunks):
            hf, c = divmod(j, chunks)
            lhs[j] = wide[:, c, hf * W : (hf + 1) * W].astype(BF16)

    def total(buffer):
        def step(i, acc):
            return acc + buffer[i].astype(F32)

        return lax.fori_loop(0, n, step, jnp.zeros((16, 2 * W), F32), unroll=8)

    def scatter(send, recv, sem):
        send[...] = wide[...].astype(BF16)
        recv[me] = send[me]
        exchange = Exchange(n, me, lambda peer: send.at[peer], recv, ssem.at[sem], rsem.at[sem])
        exchange.start()
        return exchange

    rows = lax.broadcasted_iota(jnp.int32, (16, 2 * W), 0)
    lanes = lax.broadcasted_iota(jnp.int32, (16, 2 * W), 1)

    fold(tok_ref, row_f32)
    fold(gain_ref, gain_rows)
    send1[...] = norm(row_f32[...], gain_rows[...]).astype(BF16)
    gather1 = Exchange(n, me, lambda peer: send1, recv1, ssem.at[0], rsem.at[0])
    recv1[me] = send1[...]
    pl.semaphore_wait(barrier, n - 1)
    gather1.start()

    q_in.wait()
    kv_in.wait()
    factor = (HV + ROPE) ** (-0.5)
    queries = q[...].astype(F32).T
    scores = dot(queries.astype(BF16), kv[...]) * factor
    fresh = nkv_ref[...].astype(F32)
    own = jnp.sum(queries * fresh, axis=1, keepdims=True) * factor
    usable = lax.broadcasted_iota(jnp.int32, scores.shape, 1) < len_ref[...]
    highest = jnp.maximum(
        jnp.max(jnp.where(usable, scores, -jnp.inf), axis=1, keepdims=True), own
    )
    weights = jnp.where(usable, jnp.exp(scores - highest), 0.0)
    own_weight = jnp.exp(own - highest)
    totals = jnp.sum(weights, axis=1, keepdims=True) + own_weight
    probs = (weights / totals).astype(BF16)
    probs_own = (own_weight / totals).astype(BF16).astype(F32)
    context = dot_nt(probs, kv[:LAT, :]) + probs_own * fresh[:, :LAT]
    ctx_send[...] = context.astype(BF16).astype(F32).reshape(ctx_send.shape)
    ctx_recv[me] = ctx_send[me]
    spread = Exchange(n, me, lambda peer: ctx_send.at[peer], ctx_recv, ssem.at[1], rsem.at[1])
    spread.start()

    gather1.wait_recv()
    unfold_rows(recv1)
    gate_part = jnp.zeros((n, gate.shape[0]), F32)
    up_part = jnp.zeros((n, up.shape[0]), F32)
    for j in range(2 * chunks):
        if j % chunks == 0:
            for load in projections[j // chunks]:
                load.wait()
        part = slice(j * W, (j + 1) * W)
        gate_part += dot_nt(lhs[j], gate[:, part])
        up_part += dot_nt(lhs[j], up[:, part])
    hidden = (silu(gate_part) * up_part).astype(BF16)

    spread.wait_recv()
    uv_in.wait()
    for h in range(hpd):
        flat[:, h * HV : (h + 1) * HV] = dot(ctx_recv[:, h, :].astype(BF16), uv[h]).astype(BF16)
    heads = flat[...]
    for hf in (0, 1):
        for load in branches[hf]:
            load.wait()
        for c in range(chunks):
            part = slice(hf * half + c * W, hf * half + (c + 1) * W)
            wide[:, c, hf * W : (hf + 1) * W] = dot(hidden, down[:, part]) + dot(heads, out[:, part])
    sum1 = scatter(rs1_send, rs1_recv, 2)
    fold(gain2_ref, gain_rows)
    combine = (2.5 / ids_ref.shape[1] * score_ref[...]).astype(BF16).astype(F32)
    table = jnp.zeros((16, 2 * W), F32)
    for k in range(ids_ref.shape[1]):
        table += jnp.where(lanes == ids_ref[0:1, k : k + 1], combine[0:1, k : k + 1], 0.0)
    sum1.wait_recv()
    after = row_f32[...] + total(rs1_recv)
    after = jnp.where(rows < chunks, after, 0.0).astype(BF16).astype(F32)
    unfold(after, after_ref)
    row_f32[...] = after

    moe_in = norm(after, gain_rows[...])
    send2[...] = jnp.where(rows == chunks, table, moe_in).astype(BF16)
    recv2[me] = send2[...]
    gather2 = Exchange(n, me, lambda peer: send2, recv2, ssem.at[3], rsem.at[3])
    gather2.start()
    eg_in.wait()
    eu_in.wait()
    ed_in.wait()
    gather2.wait_recv()
    unfold_rows(recv2)
    columns = wide[:, chunks, :]
    mine = lax.broadcasted_iota(jnp.int32, columns.shape, 1) == me // GROUP
    column = jnp.sum(jnp.where(mine, columns, 0.0), axis=1, keepdims=True)
    gate_part = jnp.zeros((n, eg.shape[1]), F32)
    up_part = jnp.zeros((n, eu.shape[1]), F32)
    for j in range(2 * chunks):
        part = slice(j * W, (j + 1) * W)
        gate_part += dot(lhs[j], eg[part, :])
        up_part += dot(lhs[j], eu[part, :])
    expert_hidden = (silu(gate_part) * up_part).astype(BF16)
    for hf in (0, 1):
        for c in range(chunks):
            part = slice(hf * half + c * W, hf * half + (c + 1) * W)
            wide[:, c, hf * W : (hf + 1) * W] = dot(expert_hidden, ed[:, part]) * column
    sum2 = scatter(rs2_send, rs2_recv, 4)
    for exchange in (gather1, spread, sum1, gather2):
        exchange.wait_send()
    sum2.wait_recv()
    layer = row_f32[...] + total(rs2_recv)
    unfold(layer, layer_ref)
    sum2.wait_send()


def body(
    tokens, ffn_gain, gate_weight, up_weight, down_weight, queries, kv_cache, new_kv, lengths,
    uv_weight, out_weight, moe_gain, route_ids, route_scores, expert_gate, expert_up, expert_down,
):
    n = lax.axis_size("ep")
    width = tokens.shape[1]
    hpd = uv_weight.shape[0]
    chunks = width // (2 * W)
    assert tokens.shape[0] == 1 and width % (2 * W) == 0 and chunks < 16
    big = (
        queries[0].T, kv_cache[0].T, gate_weight.T, up_weight.T, uv_weight,
        out_weight.reshape(-1, width), down_weight,
        expert_gate[0], expert_up[0], expert_down[0],
    )
    vmem = pl.BlockSpec(memory_space=pltpu.VMEM)
    slots = pltpu.VMEM((n, 16, 2 * W), BF16)
    return pl.pallas_call(
        functools.partial(kernel, n, hpd),
        out_shape=[jax.ShapeDtypeStruct((1, width), BF16)] * 2,
        in_specs=[vmem] * 7 + [pl.BlockSpec(memory_space=pl.ANY)] * len(big),
        out_specs=[vmem] * 2,
        scratch_shapes=[pltpu.VMEM(x.shape, x.dtype) for x in big]
        + [
            pltpu.VMEM((16, 2 * W), F32),
            pltpu.VMEM((16, 2 * W), F32),
            pltpu.VMEM((16, 2 * W), BF16),
            slots,
            pltpu.VMEM((n, hpd, LAT), F32),
            pltpu.VMEM((n, hpd, LAT), F32),
            slots,
            slots,
            pltpu.VMEM((16, 2 * W), BF16),
            slots,
            slots,
            slots,
            pltpu.VMEM((n, 16, 2 * W), F32),
            pltpu.VMEM((2 * chunks, n, W), BF16),
            pltpu.VMEM((n, hpd * HV), BF16),
            pltpu.SemaphoreType.DMA((len(big) + 4,)),
            pltpu.SemaphoreType.DMA((5, n)),
            pltpu.SemaphoreType.DMA((5, n)),
        ],
        compiler_params=pltpu.CompilerParams(
            collective_id=0, has_side_effects=True, vmem_limit_bytes=60 * 1024 * 1024
        ),
    )(
        tokens, ffn_gain.reshape(1, width), new_kv, lengths.reshape(1, 1),
        moe_gain.reshape(1, width), route_ids, route_scores, *big,
    )


def solution(mesh):
    in_specs = (
        P(("rep", "ep"), None),
        P(),
        P(None, "ep"),
        P(None, "ep"),
        P("ep", None),
        P(("rep", "ep"), None, None),
        P(("rep", "ep"), None, None),
        P(("rep", "ep"), None),
        P(("rep", "ep")),
        P("ep", None, None),
        P("ep", None, None),
        P(),
        P(("rep", "ep"), None),
        P(("rep", "ep"), None),
        P("ep", None, None),
        P("ep", None, None),
        P("ep", None, None),
    )
    out_specs = (P(("rep", "ep"), None), P(("rep", "ep"), None))
    return jax.shard_map(body, mesh=mesh, in_specs=in_specs, out_specs=out_specs, check_vma=False)
```
